32 devices in a mesh: dp: 8 (over z, x), tensor: 4 (over y, core).
Axes of the slice: x: 2, y: 2, z: 4, core: 2. Of those that a mesh axis runs over, the one named last changes fastest.
Arguments:
- tokens: bfloat16 [2048, 768], P('dp'), may hold values from -6 to 6
- cotangent: bfloat16 [2048, 768], P('dp'), may hold values from -6 to 6
- segment_ids: int32 [8, 256], P('dp'), may hold values from 0 to 2, never falling along the last dimension, each value on 1 to 160 neighbouring positions
- routes: int32 [2048, 2], P('dp'), may hold values from 0 to 3, all different within a row; in each aligned block of 256 rows (0 to 255, 256 to 511, ...) at most 144 rows name the same one
- buckets: int32 [256], replicated, may hold values from 0 to 31, as said below
- gain_attn: bfloat16 [768], P('dp'), may hold values from 0.5 to 1.5
- w_query: bfloat16 [768, 768], P('dp', 'tensor'), may hold values from -0.21875 to 0.21875
- w_key: bfloat16 [768, 768], P('dp', 'tensor'), may hold values from -0.21875 to 0.21875
- w_value: bfloat16 [768, 768], P('dp', 'tensor'), may hold values from -0.21875 to 0.21875
- w_out_t: bfloat16 [768, 768], P('dp', 'tensor'), may hold values from -1.25 to 1.25
- gain_moe: bfloat16 [768], P('dp'), may hold values from 0.5 to 1.5
- w_router: bfloat16 [768, 4], P('dp'), may hold values from -0.15625 to 0.15625
- w_gate: bfloat16 [4, 768, 3072], P(None, 'dp', 'tensor'), may hold values from -0.21875 to 0.21875
- w_up: bfloat16 [4, 768, 3072], P(None, 'dp', 'tensor'), may hold values from -0.21875 to 0.21875
- w_down_t: bfloat16 [4, 768, 3072], P(None, 'dp', 'tensor'), may hold values from -0.3125 to 0.3125
- bias_table: bfloat16 [12, 32], P('tensor'), may hold values from -4 to 4
Outputs:
- output: bfloat16 [2048, 768], P('dp')
- grad_tokens: bfloat16 [2048, 768], P('dp')
- grad_gain_attn: float32 [768], P('dp')
- grad_w_query: float32 [768, 768], P('dp', 'tensor')
- grad_w_key: float32 [768, 768], P('dp', 'tensor')
- grad_w_value: float32 [768, 768], P('dp', 'tensor')
- grad_w_out_t: float32 [768, 768], P('dp', 'tensor')
- grad_gain_moe: float32 [768], P('dp')
- grad_w_router: float32 [768, 4], P('dp')
- grad_w_gate: float32 [4, 768, 3072], P(None, 'dp', 'tensor')
- grad_w_up: float32 [4, 768, 3072], P(None, 'dp', 'tensor')
- grad_w_down_t: float32 [4, 768, 3072], P(None, 'dp', 'tensor')
- grad_bias_table: float32 [12, 32], P('tensor')
The draws below stay inside these ranges and needn't reach their ends.
Inputs may be any that keep to these rules, and one draw needn't show every extreme that they name: `routes`: in each sequence no expert is named by more than 144 tokens, a bound that some block reaches; a token's experts differ. `segment_ids`: never falling along a sequence. `buckets`: 0 at distance 0, never falling with the distance, 31 at distance 256 - 1.
All inputs are finite; a program needn't handle non-finite values.
Results may differ from the reference program's by a relative error of at most 0.017.
Values may be sent and summed in bfloat16 or wider, within the bound.
A program may use at most 192 MiB of HBM per device.

```python
import math
import jax
import jax.numpy as jnp
import numpy as np
from jax import lax

D = 768
H = 12
FF = 3072
EXPERTS = 4
TOP = 2
NB = 32
SEQ = 256
SEQS = 8
TOKENS = 2048
CAP = 144
HD = 768


def draw_buckets(key, part):
    key = jax.random.fold_in(key, 11)
    distance = jnp.arange(SEQ, dtype=jnp.int32)
    coin_draw = jax.random.randint(key, (SEQ,), 0, max(1, SEQ // NB))
    rising = jnp.where(distance <= NB // 4, 1, (coin_draw == 0).astype(jnp.int32))
    rising = jnp.where(distance == 0, 0, rising).astype(jnp.int32)
    bucket = jnp.minimum(jnp.cumsum(rising).astype(jnp.int32), NB - 1)
    return jnp.where(distance == SEQ - 1, NB - 1, bucket).astype(jnp.int32)


def with_spikes(result, rng, source, target, shards_of, factor):
    owner, partner = [(jnp.arange(result.shape[dim]) // (result.shape[dim] // shards_of)).reshape([-1 if axis == dim else 1 for axis in range(result.ndim)]) for dim in (source, target)]
    chosen = jax.random.permutation(rng, shards_of)[partner]
    strong = (owner == chosen) | (owner == (partner + shards_of // 2) % shards_of)
    return jnp.where(strong, factor * result, result)


def levels(rng, shape, cuts, low, high):
    level, own = 1.0, jax.random.fold_in(rng, 6)
    for dim, shards_of in cuts:
        steps = jnp.exp(jax.random.uniform(jax.random.fold_in(own, dim), (shards_of,), jnp.float32, low / len(cuts), high / len(cuts)))
        level = level * jnp.repeat(steps, shape[dim] // shards_of).reshape([-1 if axis == dim else 1 for axis in range(len(shape))])
    return level


def profile(number_of, total, bound, lean):
    portions = [(1 << 20) // math.isqrt(rank ** lean) + 1 for rank in range(2, number_of + 1)]
    rest, given = total - bound - (number_of - 1), [1] * (number_of - 1)
    while rest > 0:
        candidates = [i for i in range(number_of - 1) if given[i] < bound]
        pool, remaining = sum([portions[i] for i in candidates]), rest
        for i in candidates:
            more = min(bound - given[i], max(1, remaining * portions[i] // pool), rest)
            given[i] = given[i] + more
            rest = rest - more
    return np.array([bound] + given)


def uneven(stream_key, number_of, total, reach, slope):
    if number_of == 2:
        one = jax.random.randint(stream_key, (), max(1, total - reach), min(reach, total - 1) + 1)
        return jnp.stack([one, total - one])
    sizes = jnp.asarray(profile(number_of, total, reach, slope), jnp.int32)
    pairs = (number_of - 1) // 2
    giver, taker = sizes[1:1 + 2 * pairs:2], sizes[2:2 + 2 * pairs:2]
    room = jnp.minimum(giver - 1, reach - taker)
    shifted = jax.random.randint(jax.random.fold_in(stream_key, 1), (pairs,), 0, 1 << 20) % (room + 1)
    sizes = sizes.at[1:1 + 2 * pairs:2].set(giver - shifted).at[2:2 + 2 * pairs:2].set(taker + shifted)
    return sizes[jax.random.permutation(jax.random.fold_in(stream_key, 2), number_of)]


def shared_out(own_key, own, number, rows, number_of, top, most, skew):
    ranking = jax.random.permutation(own_key, number_of)
    heavy_load, common = load_shares(number_of, rows * top, most, skew, True), load_shares(number_of, rows * top, most, skew, False)
    places = jnp.arange(number_of)

    def named(tallies, rotation):
        used = int((tallies > 0).sum())
        fixed = max(1, used // 4)
        moved = fixed + (places - fixed + rotation * (used - fixed)) % max(1, number_of - fixed)
        return jnp.zeros((number_of,), jnp.int32).at[ranking[jnp.where(places < fixed, places, moved)]].set(jnp.asarray(tallies, jnp.int32))

    tallies = jnp.where(number % 4 == 0, named(heavy_load, number // 4), named(common, number - number // 4 - 1))
    mixed = jax.random.permutation(jax.random.fold_in(own, 3), number_of)
    giver, taker = mixed[0:number_of // 2 * 2:2], mixed[1:number_of // 2 * 2:2]
    slack = jnp.minimum(tallies[giver] - 1, most - tallies[taker]) // 2
    slack = jnp.where((giver == ranking[0]) | (taker == ranking[0]) | (tallies[taker] == 0), 0, jnp.maximum(slack, 0))
    moved = jax.random.randint(jax.random.fold_in(own, 4), (number_of // 2,), 0, 1 << 20) % (slack + 1)
    tallies = tallies.at[giver].add(-moved).at[taker].add(moved)
    members = jnp.searchsorted(jnp.cumsum(tallies), jnp.arange(rows * top), side="right").astype(jnp.int32)
    table = members.reshape(top, rows).T
    table = table[jax.random.permutation(jax.random.fold_in(own, 1), rows)]
    rotation = jax.random.randint(jax.random.fold_in(own, 2), (rows, 1), 0, top)
    return jnp.take_along_axis(table, (jnp.arange(top)[None, :] + rotation) % top, axis=1)


def load_shares(amount, total, bound, lean, full):
    loads = [(1 << 20) // math.isqrt(standing ** lean) + 1 for standing in range(1, amount + 1)]
    largest = bound if full else min(bound, max(-(-total // amount), total * loads[0] // sum(loads)))
    least = 1 if total - largest >= amount - 1 else 0
    given, rest = [largest] + [least] * (amount - 1), total - largest - least * (amount - 1)
    while rest > 0:
        candidates = [i for i in range(1, amount) if given[i] < largest] or [i for i in range(1, amount) if given[i] < bound]
        pool, left = sum([loads[i] for i in candidates]), rest
        for i in candidates:
            more = min(bound - given[i], max(1, left * loads[i] // pool), rest)
            given[i] = given[i] + more
            rest = rest - more
    return np.array(given)


def centred(own_key, dims, width, limit, split=(), kind=jnp.bfloat16):
    array = jax.random.normal(own_key, dims, jnp.float32) * width
    if len(split) > 0:
        array = levels(own_key, dims, split, -0.22, 0.18) * array
    return jnp.clip(array, min=-limit, max=limit).astype(kind)


def gaussian_with(rng, dims, spread, most, pieces, heavy, kind=jnp.bfloat16):
    values = spread * jax.random.normal(rng, dims, jnp.float32)
    if pieces:
        values = values * levels(rng, dims, pieces, -0.22, 0.18)
    return jnp.clip(with_spikes(values, jax.random.fold_in(rng, 3), *heavy), -most, most).astype(kind)


def setup_inputs(seed: int = 0) -> dict:
    splits = jax.random.split(jax.random.key(seed), 17)
    tokens = centred(splits[0], (TOKENS, D), 1.0, 6.0, ((0, 8),))
    cotangent = gaussian_with(splits[1], (TOKENS, D), 1.0, 6.0, ((0, 8),), (0, 1, 8, 2.0))
    segment_ids = jax.vmap(lambda own: jnp.searchsorted(jnp.cumsum(uneven(own, 3, SEQ, SEQ * 5 // 8, 0)), jnp.arange(SEQ), side="right"))(jax.random.split(splits[2], SEQS)).reshape((SEQS, SEQ)).astype(jnp.int32)
    routes_keys = jax.random.split(jax.random.fold_in(splits[3], 1), TOKENS // SEQ)
    routes_turns = jax.random.permutation(jax.random.fold_in(splits[3], 3), TOKENS // SEQ)
    routes = jax.vmap(lambda own, number: shared_out(jax.random.fold_in(splits[3], 2), own, number, SEQ, EXPERTS, TOP, CAP, 1))(routes_keys, routes_turns).reshape((TOKENS, TOP))
    buckets = draw_buckets(jax.random.fold_in(splits[16], 71), 0)
    gain_attn = jnp.clip(1.0 + 0.1 * jax.random.normal(splits[5], (D,), jnp.float32), 0.5, 1.5).astype(jnp.bfloat16)
    w_query = centred(splits[6], (D, HD), D ** -0.5, 0.21875, ((0, 8), (1, 4)))
    w_key = centred(splits[7], (D, HD), D ** -0.5, 0.21875, ((0, 8), (1, 4)))
    w_value = centred(splits[8], (D, HD), D ** -0.5, 0.21875, ((0, 8), (1, 4)))
    w_out_t = centred(splits[9], (D, HD), (HD * 8 // SEQ) ** -0.5, 1.25, ((0, 8), (1, 4)))
    gain_moe = jnp.clip(1.0 + 0.1 * jax.random.normal(splits[10], (D,), jnp.float32), 0.5, 1.5).astype(jnp.bfloat16)
    w_router = centred(splits[11], (D, EXPERTS), (2 * D) ** -0.5, 0.15625, ((0, 8),))
    w_gate = centred(splits[12], (EXPERTS, D, FF), D ** -0.5, 0.21875, ((1, 8), (2, 4)))
    w_up = centred(splits[13], (EXPERTS, D, FF), D ** -0.5, 0.21875, ((1, 8), (2, 4)))
    w_down_t = centred(splits[14], (EXPERTS, D, FF), (FF // 8) ** -0.5, 0.3125, ((1, 8), (2, 4)))
    bias_table = centred(splits[15], (H, NB), 1.0, 4.0, ((0, 4),))
    return dict(tokens=tokens, cotangent=cotangent, segment_ids=segment_ids, routes=routes, buckets=buckets, gain_attn=gain_attn, w_query=w_query, w_key=w_key, w_value=w_value, w_out_t=w_out_t, gain_moe=gain_moe, w_router=w_router, w_gate=w_gate, w_up=w_up, w_down_t=w_down_t, bias_table=bias_table)


EPSILON = 1e-06
NEG_FILL = -1e+30
HIGHEST = lax.Precision.HIGHEST

@jax.custom_vjp
def low(v):
    return lax.optimization_barrier(v.astype(jnp.bfloat16)).astype(jnp.float32)

@jax.custom_vjp
def low_back(v):
    return v

def low_keep(v):
    return (low(v), None)

def low_pass(kept, grad):
    return (grad,)

def back_keep(v):
    return (v, None)

def back_low(kept, grad):
    return (low(grad),)
low.defvjp(low_keep, low_pass)
low_back.defvjp(back_keep, back_low)

def matmul(left, right):
    return jnp.dot(left, right, precision=HIGHEST, preferred_element_type=jnp.float32)

def rms_scale(values, gain_vec):
    inverse = lax.rsqrt(lax.optimization_barrier(jnp.mean(values * values, axis=-1, keepdims=True)) + EPSILON)
    return values * inverse * gain_vec

def slot_tables(routes, n_experts, capacity):
    seq_len = routes.shape[0]
    position = jnp.arange(seq_len, dtype=jnp.int32)
    expert_ids = jnp.arange(n_experts, dtype=jnp.int32)
    pick_hot = (routes[:, :, None] == expert_ids[None, None, :]).astype(jnp.int32)
    chosen = lax.optimization_barrier(jnp.sum(pick_hot, axis=1)).astype(jnp.int32)
    slot_place = (jnp.cumsum(chosen, axis=0) - 1).astype(jnp.int32)
    pick_slot = lax.optimization_barrier(jnp.sum(pick_hot * slot_place[:, None, :], axis=2)).astype(jnp.int32)
    flat_slot = (routes * capacity + pick_slot).astype(jnp.int32)
    slot_ids = jnp.arange(capacity, dtype=jnp.int32)
    slot_match = ((slot_place[None, :, :] == slot_ids[:, None, None]) & (chosen[None, :, :] == 1)).astype(jnp.int32)
    slot_row = lax.optimization_barrier(jnp.sum(slot_match * position[None, :, None], axis=1)).astype(jnp.int32)
    return (pick_hot, flat_slot, slot_row)

def forward(params, tokens, segment, routes, buckets):
    gain_attn, w_query, w_key, w_value, w_out_t, gain_moe, w_router, w_gate, w_up, w_down_t, bias_table = params
    seq_len, model_width = tokens.shape
    n_heads = bias_table.shape[0]
    head_dim = w_query.shape[1] // n_heads
    normed = low(rms_scale(tokens, gain_attn))
    queries = low_back(low(matmul(normed, w_query))).reshape(seq_len, n_heads, head_dim)
    key_all = low_back(low(matmul(normed, w_key))).reshape(seq_len, n_heads, head_dim)
    values = low_back(low(matmul(normed, w_value))).reshape(seq_len, n_heads, head_dim)
    position = jnp.arange(seq_len, dtype=jnp.int32)
    offset = position[:, None] - position[None, :]
    allowed = (offset >= 0) & (segment[:, None] == segment[None, :])
    bucket_grid = jnp.take(buckets, jnp.clip(offset, 0, seq_len - 1).astype(jnp.int32))
    bias_full = jnp.take(bias_table, bucket_grid, axis=1)
    raw_scores = jnp.einsum('qhd,khd->hqk', queries, key_all, precision=HIGHEST) * head_dim ** (-0.5)
    scores = jnp.where(allowed[None, :, :], low_back(raw_scores) + bias_full, NEG_FILL)
    row_max = lax.optimization_barrier(jnp.max(scores, axis=-1, keepdims=True))
    exp_scores = jnp.exp(scores - row_max)
    prob_full = exp_scores / lax.optimization_barrier(jnp.sum(exp_scores, axis=-1, keepdims=True))
    mixed_out = jnp.einsum('hqk,khd->qhd', low(prob_full), values, precision=HIGHEST)
    mixed_out = low_back(low(mixed_out.reshape(seq_len, n_heads * head_dim)))
    residual = tokens + low_back(matmul(mixed_out, w_out_t.T))
    normed_moe = low(rms_scale(residual, gain_moe))
    router = jax.nn.softmax(low_back(matmul(normed_moe, w_router)), axis=-1)
    n_experts = w_gate.shape[0]
    pick_hot, flat_slot, slot_row = slot_tables(routes, n_experts, CAP)
    outputs = []
    for expert in range(n_experts):
        expert_rows = jnp.take(normed_moe, slot_row[:, expert], axis=0)
        gate_act = low_back(matmul(expert_rows, w_gate[expert]))
        up_act = low_back(matmul(expert_rows, w_up[expert]))
        inner_act = low(jax.nn.gelu(gate_act, approximate=False) * up_act)
        outputs.append(low_back(matmul(inner_act, w_down_t[expert].T)))
    stacked = jnp.concatenate(outputs, axis=0)
    n_picks = routes.shape[1]
    picked = jnp.take(stacked, flat_slot.reshape(-1), axis=0).reshape(seq_len, n_picks, model_width)
    gates = lax.optimization_barrier(jnp.sum(router[:, None, :] * pick_hot.astype(jnp.float32), axis=2))
    return residual + lax.optimization_barrier(jnp.sum(gates[:, :, None] * picked, axis=1))

def reference(tokens, cotangent, segment_ids, routes, buckets, gain_attn, w_query, w_key, w_value, w_out_t, gain_moe, w_router, w_gate, w_up, w_down_t, bias_table):
    params = tuple((array_in.astype(jnp.float32) for array_in in (gain_attn, w_query, w_key, w_value, w_out_t, gain_moe, w_router, w_gate, w_up, w_down_t, bias_table)))
    group_size = 8 if SEQS % 8 == 0 else 1
    n_groups = SEQS // group_size
    token_f = tokens.astype(jnp.float32).reshape(n_groups, group_size, SEQ, D)
    cot_f = cotangent.astype(jnp.float32).reshape(n_groups, group_size, SEQ, D)
    seg_groups = segment_ids.reshape(n_groups, group_size, SEQ)
    route_groups = routes.reshape(n_groups, group_size, SEQ, TOP)

    def step_group(totals, block_in):
        token_in, cot_in, seg_in, route_in = block_in

        def run_group(param_set, token_set):

            def single_seq(token_one, seg_one, route_one):
                return forward(param_set, token_one, seg_one, route_one, buckets)
            return jax.vmap(single_seq)(token_set, seg_in, route_in)
        out_set, pullback = jax.vjp(run_group, params, token_in)
        grad_params, grad_token = pullback(cot_in)
        return (jax.tree.map(jnp.add, totals, grad_params), (out_set, grad_token))
    totals, (out_all, grad_all) = lax.scan(step_group, jax.tree.map(jnp.zeros_like, params), (token_f, cot_f, seg_groups, route_groups))
    output = out_all.reshape(TOKENS, D).astype(jnp.bfloat16)
    grad_tokens = grad_all.reshape(TOKENS, D).astype(jnp.bfloat16)
    return (output, grad_tokens, totals[0], totals[1], totals[2], totals[3], totals[4], totals[5], totals[6], totals[7], totals[8], totals[9], totals[10])
```

```python
import functools

import jax
import jax.numpy as jnp
from jax import lax
from jax.experimental import pallas as pl
from jax.experimental.pallas import tpu as pltpu
from jax.sharding import PartitionSpec as P

DH = 64
CAP = 144
EPSILON = 1e-06
NEG_FILL = -1e30
HIGHEST = lax.Precision.HIGHEST
BF = jnp.bfloat16
F32 = jnp.float32
VMEM_LIMIT = 48 * 1024 * 1024


def mm(a, b, ca=1, cb=0):
    return lax.dot_general(a, b, (((ca,), (cb,)), ((), ())), preferred_element_type=F32)


def exchange_kernel(axis, n, kinds, *refs):
    m = len(kinds)
    ins, outs = refs[:m], refs[m : 2 * m]
    local_sem, send_sem, recv_sem = refs[2 * m :]
    me = lax.axis_index(axis)
    barrier = pltpu.get_barrier_semaphore()

    def greet(k, carry):
        pl.semaphore_signal(
            barrier,
            inc=1,
            device_id={axis: lax.rem(me + k, n)},
            device_id_type=pl.DeviceIdType.MESH,
        )
        return carry

    lax.fori_loop(1, n, greet, 0)

    def source(a, target):
        return ins[a] if kinds[a] == 0 else ins[a].at[target // kinds[a]]

    locals_ = [
        pltpu.make_async_copy(source(a, me), outs[a].at[me], local_sem.at[a]) for a in range(m)
    ]
    for copy in locals_:
        copy.start()
    pl.semaphore_wait(barrier, n - 1)

    def remote(a, k):
        target = lax.rem(me + k, n)
        return pltpu.make_async_remote_copy(
            src_ref=source(a, target),
            dst_ref=outs[a].at[me],
            send_sem=send_sem.at[a, k],
            recv_sem=recv_sem.at[a, k],
            device_id={axis: target},
            device_id_type=pl.DeviceIdType.MESH,
        )

    for a in range(m):

        def start(k, carry, a=a):
            remote(a, k).start()
            return carry

        lax.fori_loop(1, n, start, 0)
    for copy in locals_:
        copy.wait()
    for a in range(m):

        def finish(k, carry, a=a):
            remote(a, k).wait()
            return carry

        lax.fori_loop(1, n, finish, 0)


def exchange(arrays, kinds, axis, n, cid):
    m = len(arrays)
    shapes = [
        jax.ShapeDtypeStruct((n,) + (a.shape if k == 0 else a.shape[1:]), a.dtype)
        for a, k in zip(arrays, kinds)
    ]
    return pl.pallas_call(
        functools.partial(exchange_kernel, axis, n, kinds),
        out_shape=shapes,
        in_specs=[pl.BlockSpec(memory_space=pl.ANY)] * m,
        out_specs=[pl.BlockSpec(memory_space=pl.ANY)] * m,
        scratch_shapes=[
            pltpu.SemaphoreType.DMA((m,)),
            pltpu.SemaphoreType.DMA((m, n)),
            pltpu.SemaphoreType.DMA((m, n)),
        ],
        compiler_params=pltpu.CompilerParams(collective_id=cid, has_side_effects=True),
    )(*arrays)


def skew(x, forward):
    size = x.shape[1]
    row = lax.broadcasted_iota(jnp.int32, x.shape, 0)
    step = 1
    while step < size:
        rolled = pltpu.roll(x, step if forward else size - step, 1)
        x = jnp.where((row & step) != 0, rolled, x)
        step *= 2
    return x


def attn_fwd_kernel(q_ref, seg_row_ref, seg_col_ref, dist_ref, mixed_ref, prob_ref):
    n_heads, size = dist_ref.shape
    width = n_heads * DH
    shape = (size, size)
    row = lax.broadcasted_iota(jnp.int32, shape, 0)
    col = lax.broadcasted_iota(jnp.int32, shape, 1)
    allowed = (col <= row) & (seg_col_ref[...] == seg_row_ref[...])
    for h in range(n_heads):
        q = q_ref[:, h * DH : (h + 1) * DH]
        k = q_ref[:, width + h * DH : width + (h + 1) * DH]
        v = q_ref[:, 2 * width + h * DH : 2 * width + (h + 1) * DH]
        bias = skew(jnp.broadcast_to(dist_ref[h : h + 1, :], shape), True)
        scores = jnp.where(allowed, mm(q, k, 1, 1) * DH ** (-0.5) + bias, NEG_FILL)
        top = jnp.max(scores, axis=1, keepdims=True)
        e = jnp.exp(scores - top)
        prob = e / jnp.sum(e, axis=1, keepdims=True)
        prob_ref[h] = prob
        mixed_ref[:, h * DH : (h + 1) * DH] = mm(prob.astype(BF), v).astype(BF)


def attn_bwd_kernel(q_ref, prob_ref, dmix_ref, dq_ref, dist_ref):
    n_heads, size = dist_ref.shape
    width = n_heads * DH
    scale = DH ** (-0.5)
    for h in range(n_heads):
        q = q_ref[:, h * DH : (h + 1) * DH]
        k = q_ref[:, width + h * DH : width + (h + 1) * DH]
        v = q_ref[:, 2 * width + h * DH : 2 * width + (h + 1) * DH]
        dm = dmix_ref[:, h * DH : (h + 1) * DH]
        prob = prob_ref[h]
        d_prob = mm(dm, v, 1, 1)
        ds = prob * (d_prob - jnp.sum(prob * d_prob, axis=1, keepdims=True))
        low = ds.astype(BF)
        dq_ref[:, h * DH : (h + 1) * DH] = (mm(low, k) * scale).astype(BF)
        dq_ref[:, width + h * DH : width + (h + 1) * DH] = (mm(low, q, 0, 0) * scale).astype(BF)
        dq_ref[:, 2 * width + h * DH : 2 * width + (h + 1) * DH] = mm(
            prob.astype(BF), dm, 0, 0
        ).astype(BF)
        dist_ref[h : h + 1, :] = jnp.sum(skew(ds, False), axis=0, keepdims=True)


def local_call(kernel, out_shape, *args):
    return pl.pallas_call(
        kernel,
        out_shape=out_shape,
        compiler_params=pltpu.CompilerParams(vmem_limit_bytes=VMEM_LIMIT),
    )(*args)


def rms_scale(values, gain_vec):
    inverse = lax.rsqrt(jnp.mean(values * values, axis=-1, keepdims=True) + EPSILON)
    return values * inverse * gain_vec


def gated_unit(gate_act, up_act):
    return jax.nn.gelu(gate_act, approximate=False) * up_act


def soft_router(logits):
    return jax.nn.softmax(logits, axis=-1)


def body(
    n_dp,
    n_t,
    tokens,
    cotangent,
    segment_ids,
    routes,
    buckets,
    gain_attn,
    w_query,
    w_key,
    w_value,
    w_out_t,
    gain_moe,
    w_router,
    w_gate,
    w_up,
    w_down_t,
    bias_table,
):
    seq, width = tokens.shape
    n_exp, d_rows, hidden = w_gate.shape
    n_heads, n_buckets = bias_table.shape
    cols = n_heads * DH
    cuts = n_dp // n_exp
    part = hidden // cuts
    SDS = jax.ShapeDtypeStruct

    packed = jnp.concatenate([w_query, w_key, w_value, w_out_t], axis=1)
    smalls = jnp.concatenate(
        [gain_attn[None], gain_moe[None], w_router.T, jnp.zeros((2, d_rows), BF)], axis=0
    )
    experts_out = (
        jnp.stack([w_gate, w_up, w_down_t])
        .reshape(3, n_exp, d_rows, cuts, part)
        .transpose(1, 3, 0, 2, 4)
        .reshape(n_dp, 3, d_rows, part)
    )
    full, small_full, experts_in = exchange(
        [packed, smalls, experts_out], (0, 0, 1), "dp", n_dp, 0
    )
    full = full.reshape(width, 4 * cols)
    w_qkv, w_out = full[:, : 3 * cols], full[:, 3 * cols :]
    small_full = small_full.transpose(1, 0, 2).reshape(8, width)
    attn_gain_f = small_full[0].astype(F32)
    moe_gain_f = small_full[1].astype(F32)
    router_t = small_full[2 : 2 + n_exp]
    e_gate, e_up, e_down = [experts_in[:, i].reshape(width, part) for i in range(3)]

    token_f = tokens.astype(F32)
    normed = rms_scale(token_f, attn_gain_f).astype(BF)
    qkv = mm(normed, w_qkv).astype(BF)
    buckets_rev = jnp.roll(jnp.flip(buckets), 1)
    dist_hot = (buckets_rev[:, None] == jnp.arange(n_buckets, dtype=jnp.int32)[None, :]).astype(F32)
    dist_bias = jnp.dot(bias_table.astype(F32), dist_hot.T, precision=HIGHEST)
    mixed, prob = local_call(
        attn_fwd_kernel,
        [SDS((seq, cols), BF), SDS((n_heads, seq, seq), F32)],
        qkv,
        segment_ids,
        segment_ids.reshape(seq, 1),
        dist_bias,
    )
    attn_part = mm(mixed, w_out, 1, 1).astype(BF)
    (attn_parts,) = exchange([attn_part], (0,), "tensor", n_t, 1)
    residual = token_f + jnp.sum(attn_parts.astype(F32), axis=0)
    normed_moe = rms_scale(residual, moe_gain_f).astype(BF)
    logits = mm(normed_moe, router_t, 1, 1)
    router = soft_router(logits)

    expert_ids = jnp.arange(n_exp, dtype=jnp.int32)
    chosen = jnp.any(routes[:, :, None] == expert_ids[None, None, :], axis=1)
    chosen_b = chosen.astype(BF)
    position = jnp.arange(seq, dtype=jnp.int32)
    lower = (position[:, None] >= position[None, :]).astype(BF)
    place = mm(lower, chosen_b).astype(jnp.int32) - 1
    place = jnp.where(chosen, place, -1)
    slot_ids = jnp.arange(CAP, dtype=jnp.int32)
    pick = (place.T[:, None, :] == slot_ids[None, :, None]).astype(BF)
    gates = router * chosen.astype(F32)
    grad_final = cotangent.astype(F32)
    d_rows_all = (gates.T[:, :, None] * grad_final[None]).astype(BF)
    rows_all = jnp.concatenate(
        [jnp.broadcast_to(normed_moe[None], (n_exp, seq, width)), d_rows_all], axis=2
    )
    sends = jnp.einsum("est,etd->esd", pick, rows_all, preferred_element_type=F32).astype(BF)
    (arrived,) = exchange([sends], (cuts,), "dp", n_dp, 2)
    arrived = arrived.reshape(n_dp * CAP, 2 * width)
    rows_x, rows_d = arrived[:, :width], arrived[:, width:]

    gate_act = mm(rows_x, e_gate)
    up_act = mm(rows_x, e_up)
    inner, unit_pull = jax.vjp(gated_unit, gate_act, up_act)
    inner = inner.astype(BF)
    d_inner = mm(rows_d, e_down)
    d_gate_act, d_up_act = unit_pull(d_inner)
    d_gate_act, d_up_act = d_gate_act.astype(BF), d_up_act.astype(BF)
    part_out = mm(inner, e_down, 1, 1).astype(BF)
    part_dx = (mm(d_gate_act, e_gate, 1, 1) + mm(d_up_act, e_up, 1, 1)).astype(BF)
    returns = jnp.concatenate([part_out, part_dx], axis=1).reshape(n_dp, CAP, 2 * width)
    (returned,) = exchange([returns], (1,), "dp", n_dp, 3)
    g_down = mm(rows_d, inner, 0, 0).astype(BF)
    g_gate = mm(rows_x, d_gate_act, 0, 0).astype(BF)
    g_up = mm(rows_x, d_up_act, 0, 0).astype(BF)

    returned = returned.reshape(n_exp, cuts * CAP, 2 * width)
    pick_back = jnp.tile(pick, (1, cuts, 1))
    home = jnp.einsum("est,esd->etd", pick_back, returned, preferred_element_type=F32)
    moe_part = jnp.sum(gates.T[:, :, None] * home[:, :, :width], axis=0).astype(BF)
    d_moe_part = jnp.sum(home[:, :, width:], axis=0).astype(BF)
    d_router_part = jnp.sum(home[:, :, :width] * grad_final[None], axis=2)
    moe_parts, d_moe_parts, d_router_parts = exchange(
        [moe_part, d_moe_part, d_router_part], (0, 0, 0), "tensor", n_t, 4
    )
    moe_out = jnp.sum(moe_parts.astype(F32), axis=0)
    d_moe = jnp.sum(d_moe_parts.astype(F32), axis=0)
    d_router = jnp.sum(d_router_parts, axis=0).T
    output = (residual + moe_out).astype(BF)

    unused, soft_pull = jax.vjp(soft_router, logits)
    d_logits = soft_pull(d_router)[0].astype(BF)
    g_router = mm(d_logits, normed_moe, 0, 0)
    d_normed_moe = d_moe + mm(d_logits, router_t)
    unused, moe_pull = jax.vjp(rms_scale, residual, moe_gain_f)
    d_resid_norm, g_moe_gain = moe_pull(d_normed_moe)
    d_residual = grad_final + d_resid_norm
    d_branch = d_residual.astype(BF)
    g_out = mm(d_branch, mixed, 0, 0)
    d_mixed = mm(d_branch, w_out).astype(BF)
    d_qkv, d_dist = local_call(
        attn_bwd_kernel,
        [SDS((seq, 3 * cols), BF), SDS((n_heads, seq), F32)],
        qkv,
        prob,
        d_mixed,
    )
    g_table = jnp.dot(d_dist, dist_hot, precision=HIGHEST)
    d_normed_part = mm(d_qkv, w_qkv, 1, 1).astype(BF)
    (d_normed_parts,) = exchange([d_normed_part], (0,), "tensor", n_t, 5)
    d_normed = jnp.sum(d_normed_parts.astype(F32), axis=0)
    g_qkv = mm(normed, d_qkv, 0, 0)
    unused, first_pull = jax.vjp(rms_scale, token_f, attn_gain_f)
    d_token_norm, g_attn_gain = first_pull(d_normed)
    grad_tokens = (d_residual + d_token_norm).astype(BF)

    g_attn = jnp.concatenate([g_qkv, g_out], axis=1).astype(BF).reshape(n_dp, d_rows, 4 * cols)
    g_small = jnp.concatenate(
        [g_attn_gain[None], g_moe_gain[None], g_router, jnp.zeros((2, width), F32)], axis=0
    )
    g_small = g_small.reshape(8, n_dp, d_rows).transpose(1, 0, 2)
    g_exp = jnp.stack([g.reshape(n_dp, d_rows, part) for g in (g_gate, g_up, g_down)], axis=1)
    r_attn, r_small, r_exp, r_table = exchange(
        [g_attn, g_small, g_exp, g_table], (1, 1, 1, 0), "dp", n_dp, 6
    )
    attn_total = jnp.sum(r_attn.astype(F32), axis=0)
    small_total = jnp.sum(r_small, axis=0)
    exp_total = (
        r_exp.reshape(n_exp, cuts, 3, d_rows, part)
        .transpose(2, 0, 3, 1, 4)
        .reshape(3, n_exp, d_rows, hidden)
        .astype(F32)
    )
    return (
        output,
        grad_tokens,
        small_total[0],
        attn_total[:, :cols],
        attn_total[:, cols : 2 * cols],
        attn_total[:, 2 * cols : 3 * cols],
        attn_total[:, 3 * cols :],
        small_total[1],
        small_total[2 : 2 + n_exp].T,
        exp_total[0],
        exp_total[1],
        exp_total[2],
        jnp.sum(r_table, axis=0),
    )


def solution(mesh):
    row, both, expert = P("dp", None), P("dp", "tensor"), P(None, "dp", "tensor")
    table = P("tensor", None)
    in_specs = (row, row, row, row, P(), P("dp"), both, both, both, both, P("dp"), row)
    in_specs = in_specs + (expert, expert, expert, table)
    out_specs = (row, row, P("dp"), both, both, both, both, P("dp"), row)
    out_specs = out_specs + (expert, expert, expert, table)
    return jax.shard_map(
        functools.partial(body, mesh.shape["dp"], mesh.shape["tensor"]),
        mesh=mesh,
        in_specs=in_specs,
        out_specs=out_specs,
        check_vma=False,
    )
```

```python
import functools

import jax
import jax.numpy as jnp
from jax import lax
from jax.experimental import pallas as pl
from jax.experimental.pallas import tpu as pltpu
from jax.sharding import PartitionSpec as P

DH = 64
CAP = 144
EPSILON = 1e-06
NEG_FILL = -1e30
HIGHEST = lax.Precision.HIGHEST
BF = jnp.bfloat16
F32 = jnp.float32
VMEM_LIMIT = 48 * 1024 * 1024


def mm(a, b, ca=1, cb=0):
    return lax.dot_general(a, b, (((ca,), (cb,)), ((), ())), preferred_element_type=F32)


MESH = pl.DeviceIdType.MESH


def greet(barrier, axis, n):
    me = lax.axis_index(axis)

    def one(k, carry):
        target = lax.rem(me + k, n)
        pl.semaphore_signal(barrier, inc=1, device_id={axis: target}, device_id_type=MESH)
        return carry

    lax.fori_loop(1, n, one, 0)
    return n - 1


def each(start, stop, action):
    def one(k, carry):
        action(k)
        return carry

    lax.fori_loop(start, stop, one, 0)


def exchange_kernel(sizes, kinds, axes, *refs):
    m = len(kinds)
    ins, outs = refs[:m], refs[m : 2 * m]
    local_sem, send_sem, recv_sem = refs[2 * m :]
    barrier = pltpu.get_barrier_semaphore()
    expected = 0
    for axis in sorted(set(axes)):
        expected += greet(barrier, axis, sizes[axis])
    places = [lax.axis_index(axis) for axis in axes]

    def source(a, target):
        return ins[a] if kinds[a] == 0 else ins[a].at[target // kinds[a]]

    locals_ = [
        pltpu.make_async_copy(source(a, places[a]), outs[a].at[places[a]], local_sem.at[a])
        for a in range(m)
    ]
    for copy in locals_:
        copy.start()
    pl.semaphore_wait(barrier, expected)

    def remote(a, k):
        target = lax.rem(places[a] + k, sizes[axes[a]])
        return pltpu.make_async_remote_copy(
            src_ref=source(a, target),
            dst_ref=outs[a].at[places[a]],
            send_sem=send_sem.at[a, k],
            recv_sem=recv_sem.at[a, k],
            device_id={axes[a]: target},
            device_id_type=MESH,
        )

    for a in range(m):
        each(1, sizes[axes[a]], lambda k, a=a: remote(a, k).start())
    for copy in locals_:
        copy.wait()
    for a in range(m):
        each(1, sizes[axes[a]], lambda k, a=a: remote(a, k).wait())


def exchange(sizes, arrays, kinds, axes, cid):
    m = len(arrays)
    most = max(sizes[axis] for axis in axes)
    shapes = [
        jax.ShapeDtypeStruct((sizes[axis],) + (a.shape if k == 0 else a.shape[1:]), a.dtype)
        for a, k, axis in zip(arrays, kinds, axes)
    ]
    return pl.pallas_call(
        functools.partial(exchange_kernel, sizes, kinds, axes),
        out_shape=shapes,
        in_specs=[pl.BlockSpec(memory_space=pl.ANY)] * m,
        out_specs=[pl.BlockSpec(memory_space=pl.ANY)] * m,
        scratch_shapes=[
            pltpu.SemaphoreType.DMA((m,)),
            pltpu.SemaphoreType.DMA((m, most)),
            pltpu.SemaphoreType.DMA((m, most)),
        ],
        compiler_params=pltpu.CompilerParams(collective_id=cid, has_side_effects=True),
    )(*arrays)


def relay_setup(n):
    me, t = lax.axis_index("dp"), lax.axis_index("tensor")
    pair = t + 1 - 2 * lax.rem(t, 2)
    across = lax.rem(t + 2, 4)
    barrier = pltpu.get_barrier_semaphore()
    for target in (pair, across):
        pl.semaphore_signal(barrier, inc=1, device_id={"tensor": target}, device_id_type=MESH)
    return me, t, pair, across, barrier, 2 + greet(barrier, "dp", n)


def push(src, dst, sems, index, device):
    return pltpu.make_async_remote_copy(
        src_ref=src,
        dst_ref=dst,
        send_sem=sems[0].at[index],
        recv_sem=sems[1].at[index],
        device_id=device,
        device_id_type=MESH,
    )


def dispatch_kernel(n, cuts, in_ref, out_ref, local_sem, *sems):
    me, t, pair, across, barrier, expected = relay_setup(n)
    ring, over, near, far = [(sems[2 * i], sems[2 * i + 1]) for i in range(4)]
    own = pltpu.make_async_copy(in_ref.at[me // cuts], out_ref.at[t, me], local_sem)
    own.start()
    pl.semaphore_wait(barrier, expected)

    def first(k):
        target = lax.rem(me + k, n)
        return push(in_ref.at[target // cuts], out_ref.at[t, me], ring, k, {"dp": target})

    def place(k):
        return lax.rem(me - k + n, n)

    def cross(k):
        here = out_ref.at[t, place(k)]
        return push(here, here, over, k, {"tensor": across})

    def swap(k):
        here = out_ref.at[t, place(k)]
        return push(here, here, near, k, {"tensor": pair})

    def forward(k):
        here = out_ref.at[across, place(k)]
        return push(here, here, far, k, {"tensor": pair})

    def spread(k):
        cross(k).start()
        swap(k).start()

    def hand_on(k):
        cross(k).wait_recv()
        forward(k).start()

    each(1, n, lambda k: first(k).start())
    own.wait()
    spread(0)

    def step(k):
        first(k).wait_recv()
        spread(k)
        hand_on(k - 1)

    each(1, n, step)
    hand_on(n - 1)
    each(1, n, lambda k: first(k).wait_send())

    def finish(k):
        cross(k).wait_send()
        swap(k).wait()
        forward(k).wait()

    each(0, n, finish)


def dispatch(sends, n, cuts, cid):
    _, rows, columns = sends.shape
    return pl.pallas_call(
        functools.partial(dispatch_kernel, n, cuts),
        out_shape=jax.ShapeDtypeStruct((4, n, rows, columns), sends.dtype),
        in_specs=[pl.BlockSpec(memory_space=pl.ANY)],
        out_specs=pl.BlockSpec(memory_space=pl.ANY),
        scratch_shapes=[pltpu.SemaphoreType.DMA] + [pltpu.SemaphoreType.DMA((n,))] * 8,
        compiler_params=pltpu.CompilerParams(collective_id=cid, has_side_effects=True),
    )(sends)


def return_kernel(n, in_ref, out_ref, held, pair_in, across_in, local_sem, *sems):
    me, t, pair, across, barrier, expected = relay_setup(n)
    near, far, over, ring = [(sems[2 * i], sems[2 * i + 1]) for i in range(4)]
    loads = [
        pltpu.make_async_copy(in_ref.at[t], held.at[0], local_sem.at[0]),
        pltpu.make_async_copy(in_ref.at[across], held.at[1], local_sem.at[1]),
    ]
    for load in loads:
        load.start()
    pl.semaphore_wait(barrier, expected)
    beyond = lax.rem(pair + 2, 4)

    def place(k):
        return lax.rem(me + 1 + k, n)

    def share(k):
        s = place(k)
        return push(in_ref.at[pair, s], pair_in.at[0, s], near, k, {"tensor": pair})

    def share_far(k):
        s = place(k)
        return push(in_ref.at[beyond, s], pair_in.at[1, s], far, k, {"tensor": pair})

    def cross(k):
        s = place(k)
        return push(held.at[1, s], across_in.at[s], over, k, {"tensor": across})

    def home(k):
        s = place(k)
        return push(held.at[0, s], out_ref.at[me], ring, k, {"dp": s})

    def begin(k):
        share_far(k).start()
        share(k).start()

    def sum_far(k):
        s = place(k)
        share_far(k).wait_recv()
        held[1, s] = (held[1, s].astype(F32) + pair_in[1, s].astype(F32)).astype(BF)
        cross(k).start()

    def sum_own(k):
        s = place(k)
        share(k).wait_recv()
        cross(k).wait_recv()
        total = held[0, s].astype(F32) + pair_in[0, s].astype(F32) + across_in[s].astype(F32)
        held[0, s] = total.astype(BF)

    each(0, n, begin)
    for load in loads:
        load.wait()
    sum_far(0)

    def step(k):
        sum_far(k)
        sum_own(k - 1)
        home(k - 1).start()

    each(1, n, step)
    sum_own(n - 1)
    own = pltpu.make_async_copy(held.at[0, me], out_ref.at[me], local_sem.at[0])
    own.start()
    own.wait()
    each(0, n - 1, lambda k: home(k).wait())

    def finish(k):
        share(k).wait_send()
        share_far(k).wait_send()
        cross(k).wait_send()

    each(0, n, finish)


def send_home(parts, n, cid):
    _, _, rows, columns = parts.shape
    block = (n, rows, columns)
    return pl.pallas_call(
        functools.partial(return_kernel, n),
        out_shape=jax.ShapeDtypeStruct(block, parts.dtype),
        in_specs=[pl.BlockSpec(memory_space=pl.ANY)],
        out_specs=pl.BlockSpec(memory_space=pl.ANY),
        scratch_shapes=[
            pltpu.VMEM((2,) + block, parts.dtype),
            pltpu.VMEM((2,) + block, parts.dtype),
            pltpu.VMEM(block, parts.dtype),
            pltpu.SemaphoreType.DMA((2,)),
        ]
        + [pltpu.SemaphoreType.DMA((n,))] * 8,
        compiler_params=pltpu.CompilerParams(
            collective_id=cid, has_side_effects=True, vmem_limit_bytes=VMEM_LIMIT
        ),
    )(parts)


def skew(x, forward):
    size = x.shape[1]
    row = lax.broadcasted_iota(jnp.int32, x.shape, 0)
    step = 1
    while step < size:
        rolled = pltpu.roll(x, step if forward else size - step, 1)
        x = jnp.where((row & step) != 0, rolled, x)
        step *= 2
    return x


def attn_fwd_kernel(q_ref, seg_row_ref, seg_col_ref, dist_ref, mixed_ref, prob_ref):
    n_heads, size = dist_ref.shape
    width = n_heads * DH
    shape = (size, size)
    row = lax.broadcasted_iota(jnp.int32, shape, 0)
    col = lax.broadcasted_iota(jnp.int32, shape, 1)
    allowed = (col <= row) & (seg_col_ref[...] == seg_row_ref[...])
    for h in range(n_heads):
        q = q_ref[:, h * DH : (h + 1) * DH]
        k = q_ref[:, width + h * DH : width + (h + 1) * DH]
        v = q_ref[:, 2 * width + h * DH : 2 * width + (h + 1) * DH]
        bias = skew(jnp.broadcast_to(dist_ref[h : h + 1, :], shape), True)
        scores = jnp.where(allowed, mm(q, k, 1, 1) * DH ** (-0.5) + bias, NEG_FILL)
        top = jnp.max(scores, axis=1, keepdims=True)
        e = jnp.exp(scores - top)
        prob = e / jnp.sum(e, axis=1, keepdims=True)
        prob_ref[h] = prob
        mixed_ref[:, h * DH : (h + 1) * DH] = mm(prob.astype(BF), v).astype(BF)


def attn_bwd_kernel(q_ref, prob_ref, dmix_ref, dq_ref, dist_ref):
    n_heads, size = dist_ref.shape
    width = n_heads * DH
    scale = DH ** (-0.5)
    for h in range(n_heads):
        q = q_ref[:, h * DH : (h + 1) * DH]
        k = q_ref[:, width + h * DH : width + (h + 1) * DH]
        v = q_ref[:, 2 * width + h * DH : 2 * width + (h + 1) * DH]
        dm = dmix_ref[:, h * DH : (h + 1) * DH]
        prob = prob_ref[h]
        d_prob = mm(dm, v, 1, 1)
        ds = prob * (d_prob - jnp.sum(prob * d_prob, axis=1, keepdims=True))
        low = ds.astype(BF)
        dq_ref[:, h * DH : (h + 1) * DH] = (mm(low, k) * scale).astype(BF)
        dq_ref[:, width + h * DH : width + (h + 1) * DH] = (mm(low, q, 0, 0) * scale).astype(BF)
        dq_ref[:, 2 * width + h * DH : 2 * width + (h + 1) * DH] = mm(
            prob.astype(BF), dm, 0, 0
        ).astype(BF)
        dist_ref[h : h + 1, :] = jnp.sum(skew(ds, False), axis=0, keepdims=True)


def local_call(kernel, out_shape, *args):
    return pl.pallas_call(
        kernel,
        out_shape=out_shape,
        compiler_params=pltpu.CompilerParams(vmem_limit_bytes=VMEM_LIMIT),
    )(*args)


def rms_scale(values, gain_vec):
    inverse = lax.rsqrt(jnp.mean(values * values, axis=-1, keepdims=True) + EPSILON)
    return values * inverse * gain_vec


def gated_unit(gate_act, up_act):
    return jax.nn.gelu(gate_act, approximate=False) * up_act


def soft_router(logits):
    return jax.nn.softmax(logits, axis=-1)


def body(
    n_dp,
    n_t,
    tokens,
    cotangent,
    segment_ids,
    routes,
    buckets,
    gain_attn,
    w_query,
    w_key,
    w_value,
    w_out_t,
    gain_moe,
    w_router,
    w_gate,
    w_up,
    w_down_t,
    bias_table,
):
    seq, width = tokens.shape
    n_exp, d_rows, hidden = w_gate.shape
    n_heads, n_buckets = bias_table.shape
    cols = n_heads * DH
    cuts = n_dp // n_exp
    part = hidden // cuts
    sizes = {"dp": n_dp, "tensor": n_t}
    turn = lax.axis_index("tensor")
    SDS = jax.ShapeDtypeStruct

    packed = jnp.concatenate([w_query, w_key, w_value, w_out_t], axis=1)
    smalls = jnp.concatenate(
        [gain_attn[None], gain_moe[None], w_router.T, jnp.zeros((2, d_rows), BF)], axis=0
    )
    experts_out = [
        jnp.stack([w[:, :, c * part : (c + 1) * part] for c in range(cuts)], axis=1).reshape(
            n_dp, d_rows, part
        )
        for w in (w_gate, w_up, w_down_t)
    ]
    full, small_full = exchange(sizes, [packed, smalls], (0, 0), ("dp", "dp"), 0)
    full = full.reshape(width, 4 * cols)
    w_qkv, w_out = full[:, : 3 * cols], full[:, 3 * cols :]
    small_full = small_full.transpose(1, 0, 2).reshape(8, width)
    attn_gain_f = small_full[0].astype(F32)
    moe_gain_f = small_full[1].astype(F32)
    router_t = small_full[2 : 2 + n_exp]

    token_f = tokens.astype(F32)
    normed = rms_scale(token_f, attn_gain_f).astype(BF)
    qkv = mm(normed, w_qkv).astype(BF)
    buckets_rev = jnp.roll(jnp.flip(buckets), 1)
    dist_hot = (buckets_rev[:, None] == jnp.arange(n_buckets, dtype=jnp.int32)[None, :]).astype(F32)
    dist_bias = jnp.dot(bias_table.astype(F32), dist_hot.T, precision=HIGHEST)
    mixed, prob = local_call(
        attn_fwd_kernel,
        [SDS((seq, cols), BF), SDS((n_heads, seq, seq), F32)],
        qkv,
        segment_ids,
        segment_ids.reshape(seq, 1),
        dist_bias,
    )
    attn_part = mm(mixed, w_out, 1, 1).astype(BF)
    attn_parts, *experts_in = exchange(
        sizes, [attn_part] + experts_out, (0, 1, 1, 1), ("tensor", "dp", "dp", "dp"), 1
    )
    e_gate, e_up, e_down = [w.reshape(width, part) for w in experts_in]
    residual = token_f + jnp.sum(attn_parts.astype(F32), axis=0)
    normed_moe = rms_scale(residual, moe_gain_f).astype(BF)
    logits = mm(normed_moe, router_t, 1, 1)
    router = soft_router(logits)

    expert_ids = jnp.arange(n_exp, dtype=jnp.int32)
    chosen = jnp.any(routes[:, :, None] == expert_ids[None, None, :], axis=1)
    chosen_b = chosen.astype(BF)
    position = jnp.arange(seq, dtype=jnp.int32)
    lower = (position[:, None] >= position[None, :]).astype(BF)
    place = mm(lower, chosen_b).astype(jnp.int32) - 1
    place = jnp.where(chosen, place, -1)
    slot_ids = jnp.arange(CAP, dtype=jnp.int32)
    pick = (place.T[:, None, :] == slot_ids[None, :, None]).astype(BF)
    gates = router * chosen.astype(F32)
    grad_final = cotangent.astype(F32)
    quarter = width // 2
    column = lax.rem(turn, 2) * quarter
    is_out = turn < 2
    grad_slice = lax.dynamic_slice_in_dim(grad_final, column, quarter, 1)
    moe_slice = lax.dynamic_slice_in_dim(normed_moe, column, quarter, 1)
    rows_all = jnp.where(is_out, moe_slice[None], (gates.T[:, :, None] * grad_slice[None]).astype(BF))
    sends = jnp.einsum("est,etd->esd", pick, rows_all, preferred_element_type=F32).astype(BF)
    arrived = dispatch(sends, n_dp, cuts, 2).reshape(4, n_dp * CAP, quarter)
    rows_x = jnp.concatenate([arrived[0], arrived[1]], axis=1)
    rows_d = jnp.concatenate([arrived[2], arrived[3]], axis=1)

    gate_act = mm(rows_x, e_gate)
    up_act = mm(rows_x, e_up)
    inner, unit_pull = jax.vjp(gated_unit, gate_act, up_act)
    inner = inner.astype(BF)
    d_inner = mm(rows_d, e_down)
    d_gate_act, d_up_act = unit_pull(d_inner)
    d_gate_act, d_up_act = d_gate_act.astype(BF), d_up_act.astype(BF)
    part_out = mm(inner, e_down, 1, 1).astype(BF)
    part_dx = (mm(d_gate_act, e_gate, 1, 1) + mm(d_up_act, e_up, 1, 1)).astype(BF)
    returns = jnp.stack(
        [p[:, c : c + quarter] for p in (part_out, part_dx) for c in (0, quarter)]
    ).reshape(4, n_dp, CAP, quarter)
    returned = send_home(returns, n_dp, 3)
    g_down = mm(rows_d, inner, 0, 0).astype(BF)
    g_gate = mm(rows_x, d_gate_act, 0, 0).astype(BF)
    g_up = mm(rows_x, d_up_act, 0, 0).astype(BF)

    returned = returned.reshape(n_exp, cuts * CAP, quarter)
    pick_back = jnp.tile(pick, (1, cuts, 1))
    home = jnp.einsum("est,esd->etd", pick_back, returned, preferred_element_type=F32)
    scaled = jnp.where(is_out, gates.T, 1.0)
    layer_part = jnp.sum(scaled[:, :, None] * home, axis=0).astype(BF)
    d_router_part = jnp.where(is_out, jnp.sum(home * grad_slice[None], axis=2), 0.0)
    g_exp = [g.reshape(n_dp, d_rows, part) for g in (g_gate, g_up, g_down)]
    layer_parts, d_router_parts, *r_exp = exchange(
        sizes,
        [layer_part, d_router_part] + g_exp,
        (0, 0, 1, 1, 1),
        ("tensor", "tensor", "dp", "dp", "dp"),
        4,
    )
    layer_parts = layer_parts.astype(F32)
    moe_out = jnp.concatenate([layer_parts[0], layer_parts[1]], axis=1)
    d_moe = jnp.concatenate([layer_parts[2], layer_parts[3]], axis=1)
    d_router = jnp.sum(d_router_parts, axis=0).T
    output = (residual + moe_out).astype(BF)

    unused, soft_pull = jax.vjp(soft_router, logits)
    d_logits = soft_pull(d_router)[0].astype(BF)
    g_router = mm(d_logits, normed_moe, 0, 0)
    d_normed_moe = d_moe + mm(d_logits, router_t)
    unused, moe_pull = jax.vjp(rms_scale, residual, moe_gain_f)
    d_resid_norm, g_moe_gain = moe_pull(d_normed_moe)
    d_residual = grad_final + d_resid_norm
    d_branch = d_residual.astype(BF)
    g_out = mm(d_branch, mixed, 0, 0)
    d_mixed = mm(d_branch, w_out).astype(BF)
    d_qkv, d_dist = local_call(
        attn_bwd_kernel,
        [SDS((seq, 3 * cols), BF), SDS((n_heads, seq), F32)],
        qkv,
        prob,
        d_mixed,
    )
    g_table = jnp.dot(d_dist, dist_hot, precision=HIGHEST)
    d_normed_part = mm(d_qkv, w_qkv, 1, 1).astype(BF)
    g_qkv = mm(normed, d_qkv, 0, 0)
    g_attn = jnp.concatenate([g_qkv, g_out], axis=1).astype(BF).reshape(n_dp, d_rows, 4 * cols)
    g_small = jnp.concatenate(
        [g_moe_gain[None], g_router, jnp.zeros((7 - n_exp, width), F32)], axis=0
    )
    g_small = g_small.reshape(8, n_dp, d_rows).transpose(1, 0, 2)
    d_normed_parts, r_attn, r_small, r_table = exchange(
        sizes,
        [d_normed_part, g_attn, g_small, g_table],
        (0, 1, 1, 0),
        ("tensor", "dp", "dp", "dp"),
        5,
    )
    d_normed = jnp.sum(d_normed_parts.astype(F32), axis=0)
    unused, first_pull = jax.vjp(rms_scale, token_f, attn_gain_f)
    d_token_norm, g_attn_gain = first_pull(d_normed)
    grad_tokens = (d_residual + d_token_norm).astype(BF)
    (r_gain,) = exchange(sizes, [g_attn_gain.reshape(n_dp, 1, d_rows)], (1,), ("dp",), 6)
    attn_total = jnp.sum(r_attn.astype(F32), axis=0)
    small_total = jnp.sum(r_small, axis=0)
    exp_total = []
    for r in r_exp:
        r = r.reshape(n_exp, cuts, d_rows, part)
        exp_total.append(jnp.concatenate([r[:, c] for c in range(cuts)], axis=2).astype(F32))
    return (
        output,
        grad_tokens,
        jnp.sum(r_gain, axis=0)[0],
        attn_total[:, :cols],
        attn_total[:, cols : 2 * cols],
        attn_total[:, 2 * cols : 3 * cols],
        attn_total[:, 3 * cols :],
        small_total[0],
        small_total[1 : 1 + n_exp].T,
        exp_total[0],
        exp_total[1],
        exp_total[2],
        jnp.sum(r_table, axis=0),
    )


def solution(mesh):
    row, both, expert = P("dp", None), P("dp", "tensor"), P(None, "dp", "tensor")
    table = P("tensor", None)
    in_specs = (row, row, row, row, P(), P("dp"), both, both, both, both, P("dp"), row)
    in_specs = in_specs + (expert, expert, expert, table)
    out_specs = (row, row, P("dp"), both, both, both, both, P("dp"), row)
    out_specs = out_specs + (expert, expert, expert, table)
    return jax.shard_map(
        functools.partial(body, mesh.shape["dp"], mesh.shape["tensor"]),
        mesh=mesh,
        in_specs=in_specs,
        out_specs=out_specs,
        check_vma=False,
    )
```

```python
import functools

import jax
import jax.numpy as jnp
from jax import lax
from jax.experimental import pallas as pl
from jax.experimental.pallas import tpu as pltpu
from jax.sharding import PartitionSpec as P

DH = 64
CAP = 144
EPSILON = 1e-06
NEG_FILL = -1e30
HIGHEST = lax.Precision.HIGHEST
BF = jnp.bfloat16
F32 = jnp.float32
VMEM_LIMIT = 48 * 1024 * 1024


def mm(a, b, ca=1, cb=0):
    return lax.dot_general(a, b, (((ca,), (cb,)), ((), ())), preferred_element_type=F32)


MESH = pl.DeviceIdType.MESH


def greet(barrier, axis, n):
    me = lax.axis_index(axis)

    def one(k, carry):
        target = lax.rem(me + k, n)
        pl.semaphore_signal(barrier, inc=1, device_id={axis: target}, device_id_type=MESH)
        return carry

    lax.fori_loop(1, n, one, 0)
    return n - 1


def each(start, stop, action):
    def one(k, carry):
        action(k)
        return carry

    lax.fori_loop(start, stop, one, 0)


def fold_plan(n, in_ref, out_ref, held, came, load_sem, own_sem, *sems):
    near, ring = sems[:2], sems[2:]
    half = n // 2
    me = lax.axis_index("dp")
    low, high = lax.rem(me, 2), me // 2
    other = 1 - low

    def place(k):
        return lax.rem(high + 1 + k, half)

    def load(k):
        s = place(k)
        return pltpu.make_async_copy(in_ref.at[2 * s + low], held.at[s], load_sem.at[k])

    def share(k):
        s = place(k)
        target = {"dp": 2 * high + other}
        return push(in_ref.at[2 * s + other], came.at[s], near, k, target)

    def send(k):
        s = place(k)
        return push(held.at[s], out_ref.at[high], ring, k, {"dp": 2 * s + low})

    def begin(k):
        load(k).start()
        share(k).start()

    def add(k):
        s = place(k)
        load(k).wait()
        share(k).wait_recv()
        held[s] = (held[s].astype(F32) + came[s].astype(F32)).astype(BF)

    def step(k):
        add(k)
        send(k).start()

    def start():
        each(0, half, begin)

    def run():
        each(0, half - 1, step)
        add(half - 1)
        own = pltpu.make_async_copy(held.at[high], out_ref.at[high], own_sem)
        own.start()
        own.wait()

    def finish():
        each(0, half - 1, lambda k: send(k).wait())
        each(0, half, lambda k: share(k).wait_send())

    return start, run, finish


def exchange_kernel(sizes, kinds, axes, fold, *refs):
    m = len(kinds)
    f = m + fold
    ins, outs = refs[:m], refs[f : f + m]
    local_sem, send_sem, recv_sem = refs[2 * f : 2 * f + 3]
    if fold:
        plan = fold_plan(sizes["dp"], refs[m], refs[f + m], *refs[2 * f + 3 :])
    barrier = pltpu.get_barrier_semaphore()
    expected = 0
    for axis in sorted(set(axes)):
        expected += greet(barrier, axis, sizes[axis])
    places = [lax.axis_index(axis) for axis in axes]

    def source(a, target):
        return ins[a] if kinds[a] == 0 else ins[a].at[target // kinds[a]]

    locals_ = [
        pltpu.make_async_copy(source(a, places[a]), outs[a].at[places[a]], local_sem.at[a])
        for a in range(m)
    ]
    for copy in locals_:
        copy.start()
    pl.semaphore_wait(barrier, expected)

    def remote(a, k):
        target = lax.rem(places[a] + k, sizes[axes[a]])
        return pltpu.make_async_remote_copy(
            src_ref=source(a, target),
            dst_ref=outs[a].at[places[a]],
            send_sem=send_sem.at[a, k],
            recv_sem=recv_sem.at[a, k],
            device_id={axes[a]: target},
            device_id_type=MESH,
        )

    if fold:
        plan[0]()
    for a in range(m):
        each(1, sizes[axes[a]], lambda k, a=a: remote(a, k).start())
    if fold:
        plan[1]()
    for copy in locals_:
        copy.wait()
    if fold:
        plan[2]()
    for a in range(m):
        each(1, sizes[axes[a]], lambda k, a=a: remote(a, k).wait())


def exchange(sizes, arrays, kinds, axes, cid, fold=None):
    m = len(arrays)
    most = max(sizes[axis] for axis in axes)
    shapes = [
        jax.ShapeDtypeStruct((sizes[axis],) + (a.shape if k == 0 else a.shape[1:]), a.dtype)
        for a, k, axis in zip(arrays, kinds, axes)
    ]
    scratch = [
        pltpu.SemaphoreType.DMA((m,)),
        pltpu.SemaphoreType.DMA((m, most)),
        pltpu.SemaphoreType.DMA((m, most)),
    ]
    if fold is not None:
        half = sizes["dp"] // 2
        block = (half,) + fold.shape[1:]
        arrays = arrays + [fold]
        shapes = shapes + [jax.ShapeDtypeStruct(block, fold.dtype)]
        scratch = scratch + [pltpu.VMEM(block, fold.dtype)] * 2
        scratch = scratch + [pltpu.SemaphoreType.DMA((half,)), pltpu.SemaphoreType.DMA]
        scratch = scratch + [pltpu.SemaphoreType.DMA((half,))] * 4
    return pl.pallas_call(
        functools.partial(exchange_kernel, sizes, kinds, axes, int(fold is not None)),
        out_shape=shapes,
        in_specs=[pl.BlockSpec(memory_space=pl.ANY)] * len(arrays),
        out_specs=[pl.BlockSpec(memory_space=pl.ANY)] * len(arrays),
        scratch_shapes=scratch,
        compiler_params=pltpu.CompilerParams(
            collective_id=cid, has_side_effects=True, vmem_limit_bytes=VMEM_LIMIT
        ),
    )(*arrays)


def relay_setup(n):
    me, t = lax.axis_index("dp"), lax.axis_index("tensor")
    pair = t + 1 - 2 * lax.rem(t, 2)
    across = lax.rem(t + 2, 4)
    barrier = pltpu.get_barrier_semaphore()
    for target in (pair, across):
        pl.semaphore_signal(barrier, inc=1, device_id={"tensor": target}, device_id_type=MESH)
    return me, t, pair, across, barrier, 2 + greet(barrier, "dp", n)


def push(src, dst, sems, index, device):
    return pltpu.make_async_remote_copy(
        src_ref=src,
        dst_ref=dst,
        send_sem=sems[0].at[index],
        recv_sem=sems[1].at[index],
        device_id=device,
        device_id_type=MESH,
    )


def gather_kernel(n, m, *refs):
    ins, outs = refs[:m], refs[m : 2 * m]
    local_sem = refs[2 * m]
    ring, near = refs[2 * m + 1 : 2 * m + 3], refs[2 * m + 3 :]
    me = lax.axis_index("dp")
    partner = me + 1 - 2 * lax.rem(me, 2)
    barrier = pltpu.get_barrier_semaphore()
    expected = greet(barrier, "dp", n)
    locals_ = [
        pltpu.make_async_copy(ins[a], outs[a].at[me], local_sem.at[a]) for a in range(m)
    ]
    for copy in locals_:
        copy.start()
    pl.semaphore_wait(barrier, expected)

    def first(a, k):
        target = lax.rem(me + 2 * k, n)
        return push(ins[a], outs[a].at[me], ring, (a, k), {"dp": target})

    def own(a):
        return push(ins[a], outs[a].at[me], near, (a, 0), {"dp": partner})

    def forward(a, k):
        here = outs[a].at[lax.rem(me - 2 * k + n, n)]
        return push(here, here, near, (a, k), {"dp": partner})

    for a in range(m):
        each(1, n // 2, lambda k, a=a: first(a, k).start())
        own(a).start()

    def step(a, k):
        first(a, k).wait_recv()
        forward(a, k).start()

    for a in range(m):
        each(1, n // 2, lambda k, a=a: step(a, k))
    for copy in locals_:
        copy.wait()
    for a in range(m):
        own(a).wait()

        def finish(k, a=a):
            first(a, k).wait_send()
            forward(a, k).wait()

        each(1, n // 2, finish)


def gather(arrays, n, cid):
    m = len(arrays)
    return pl.pallas_call(
        functools.partial(gather_kernel, n, m),
        out_shape=[jax.ShapeDtypeStruct((n,) + a.shape, a.dtype) for a in arrays],
        in_specs=[pl.BlockSpec(memory_space=pl.ANY)] * m,
        out_specs=[pl.BlockSpec(memory_space=pl.ANY)] * m,
        scratch_shapes=[pltpu.SemaphoreType.DMA((m,))]
        + [pltpu.SemaphoreType.DMA((m, n // 2))] * 4,
        compiler_params=pltpu.CompilerParams(collective_id=cid, has_side_effects=True),
    )(*arrays)


def dispatch_kernel(n, cuts, in_ref, out_ref, local_sem, *sems):
    me, t, pair, across, barrier, expected = relay_setup(n)
    ring, over, near, far = [(sems[2 * i], sems[2 * i + 1]) for i in range(4)]
    own = pltpu.make_async_copy(in_ref.at[me // cuts], out_ref.at[t, me], local_sem)
    own.start()
    pl.semaphore_wait(barrier, expected)

    def first(k):
        target = lax.rem(me + k, n)
        return push(in_ref.at[target // cuts], out_ref.at[t, me], ring, k, {"dp": target})

    def place(k):
        return lax.rem(me - k + n, n)

    def cross(k):
        here = out_ref.at[t, place(k)]
        return push(here, here, over, k, {"tensor": across})

    def swap(k):
        here = out_ref.at[t, place(k)]
        return push(here, here, near, k, {"tensor": pair})

    def forward(k):
        here = out_ref.at[across, place(k)]
        return push(here, here, far, k, {"tensor": pair})

    def spread(k):
        cross(k).start()
        swap(k).start()

    def hand_on(k):
        cross(k).wait_recv()
        forward(k).start()

    each(1, n, lambda k: first(k).start())
    own.wait()
    spread(0)

    def step(k):
        first(k).wait_recv()
        spread(k)
        hand_on(k - 1)

    each(1, n, step)
    hand_on(n - 1)
    each(1, n, lambda k: first(k).wait_send())

    def finish(k):
        cross(k).wait_send()
        swap(k).wait()
        forward(k).wait()

    each(0, n, finish)


def dispatch(sends, n, cuts, cid):
    _, rows, columns = sends.shape
    return pl.pallas_call(
        functools.partial(dispatch_kernel, n, cuts),
        out_shape=jax.ShapeDtypeStruct((4, n, rows, columns), sends.dtype),
        in_specs=[pl.BlockSpec(memory_space=pl.ANY)],
        out_specs=pl.BlockSpec(memory_space=pl.ANY),
        scratch_shapes=[pltpu.SemaphoreType.DMA] + [pltpu.SemaphoreType.DMA((n,))] * 8,
        compiler_params=pltpu.CompilerParams(collective_id=cid, has_side_effects=True),
    )(sends)


def return_kernel(n, in_ref, out_ref, held, pair_in, across_in, local_sem, *sems):
    me, t, pair, across, barrier, expected = relay_setup(n)
    near, far, over, ring = [(sems[2 * i], sems[2 * i + 1]) for i in range(4)]
    loads = [
        pltpu.make_async_copy(in_ref.at[t], held.at[0], local_sem.at[0]),
        pltpu.make_async_copy(in_ref.at[across], held.at[1], local_sem.at[1]),
    ]
    for load in loads:
        load.start()
    pl.semaphore_wait(barrier, expected)
    beyond = lax.rem(pair + 2, 4)

    def place(k):
        return lax.rem(me + 1 + k, n)

    def share(k):
        s = place(k)
        return push(in_ref.at[pair, s], pair_in.at[0, s], near, k, {"tensor": pair})

    def share_far(k):
        s = place(k)
        return push(in_ref.at[beyond, s], pair_in.at[1, s], far, k, {"tensor": pair})

    def cross(k):
        s = place(k)
        return push(held.at[1, s], across_in.at[s], over, k, {"tensor": across})

    def home(k):
        s = place(k)
        return push(held.at[0, s], out_ref.at[me], ring, k, {"dp": s})

    def begin(k):
        share_far(k).start()
        share(k).start()

    def sum_far(k):
        s = place(k)
        share_far(k).wait_recv()
        held[1, s] = (held[1, s].astype(F32) + pair_in[1, s].astype(F32)).astype(BF)
        cross(k).start()

    def sum_own(k):
        s = place(k)
        share(k).wait_recv()
        cross(k).wait_recv()
        total = held[0, s].astype(F32) + pair_in[0, s].astype(F32) + across_in[s].astype(F32)
        held[0, s] = total.astype(BF)

    each(0, n, begin)
    for load in loads:
        load.wait()
    sum_far(0)

    def step(k):
        sum_far(k)
        sum_own(k - 1)
        home(k - 1).start()

    each(1, n, step)
    sum_own(n - 1)
    own = pltpu.make_async_copy(held.at[0, me], out_ref.at[me], local_sem.at[0])
    own.start()
    own.wait()
    each(0, n - 1, lambda k: home(k).wait())

    def finish(k):
        share(k).wait_send()
        share_far(k).wait_send()
        cross(k).wait_send()

    each(0, n, finish)


def send_home(parts, n, cid):
    _, _, rows, columns = parts.shape
    block = (n, rows, columns)
    return pl.pallas_call(
        functools.partial(return_kernel, n),
        out_shape=jax.ShapeDtypeStruct(block, parts.dtype),
        in_specs=[pl.BlockSpec(memory_space=pl.ANY)],
        out_specs=pl.BlockSpec(memory_space=pl.ANY),
        scratch_shapes=[
            pltpu.VMEM((2,) + block, parts.dtype),
            pltpu.VMEM((2,) + block, parts.dtype),
            pltpu.VMEM(block, parts.dtype),
            pltpu.SemaphoreType.DMA((2,)),
        ]
        + [pltpu.SemaphoreType.DMA((n,))] * 8,
        compiler_params=pltpu.CompilerParams(
            collective_id=cid, has_side_effects=True, vmem_limit_bytes=VMEM_LIMIT
        ),
    )(parts)


def skew(x, forward):
    size = x.shape[1]
    row = lax.broadcasted_iota(jnp.int32, x.shape, 0)
    step = 1
    while step < size:
        rolled = pltpu.roll(x, step if forward else size - step, 1)
        x = jnp.where((row & step) != 0, rolled, x)
        step *= 2
    return x


def attn_fwd_kernel(q_ref, seg_row_ref, seg_col_ref, dist_ref, mixed_ref, prob_ref):
    n_heads, size = dist_ref.shape
    width = n_heads * DH
    shape = (size, size)
    row = lax.broadcasted_iota(jnp.int32, shape, 0)
    col = lax.broadcasted_iota(jnp.int32, shape, 1)
    allowed = (col <= row) & (seg_col_ref[...] == seg_row_ref[...])
    for h in range(n_heads):
        q = q_ref[:, h * DH : (h + 1) * DH]
        k = q_ref[:, width + h * DH : width + (h + 1) * DH]
        v = q_ref[:, 2 * width + h * DH : 2 * width + (h + 1) * DH]
        bias = skew(jnp.broadcast_to(dist_ref[h : h + 1, :], shape), True)
        scores = jnp.where(allowed, mm(q, k, 1, 1) * DH ** (-0.5) + bias, NEG_FILL)
        top = jnp.max(scores, axis=1, keepdims=True)
        e = jnp.exp(scores - top)
        prob = e / jnp.sum(e, axis=1, keepdims=True)
        prob_ref[h] = prob
        mixed_ref[:, h * DH : (h + 1) * DH] = mm(prob.astype(BF), v).astype(BF)


def attn_bwd_kernel(q_ref, prob_ref, dmix_ref, dq_ref, dist_ref):
    n_heads, size = dist_ref.shape
    width = n_heads * DH
    scale = DH ** (-0.5)
    for h in range(n_heads):
        q = q_ref[:, h * DH : (h + 1) * DH]
        k = q_ref[:, width + h * DH : width + (h + 1) * DH]
        v = q_ref[:, 2 * width + h * DH : 2 * width + (h + 1) * DH]
        dm = dmix_ref[:, h * DH : (h + 1) * DH]
        prob = prob_ref[h]
        d_prob = mm(dm, v, 1, 1)
        ds = prob * (d_prob - jnp.sum(prob * d_prob, axis=1, keepdims=True))
        low = ds.astype(BF)
        dq_ref[:, h * DH : (h + 1) * DH] = (mm(low, k) * scale).astype(BF)
        dq_ref[:, width + h * DH : width + (h + 1) * DH] = (mm(low, q, 0, 0) * scale).astype(BF)
        dq_ref[:, 2 * width + h * DH : 2 * width + (h + 1) * DH] = mm(
            prob.astype(BF), dm, 0, 0
        ).astype(BF)
        dist_ref[h : h + 1, :] = jnp.sum(skew(ds, False), axis=0, keepdims=True)


def local_call(kernel, out_shape, *args):
    return pl.pallas_call(
        kernel,
        out_shape=out_shape,
        compiler_params=pltpu.CompilerParams(vmem_limit_bytes=VMEM_LIMIT),
    )(*args)


def rms_scale(values, gain_vec):
    inverse = lax.rsqrt(jnp.mean(values * values, axis=-1, keepdims=True) + EPSILON)
    return values * inverse * gain_vec


def gated_unit(gate_act, up_act):
    return jax.nn.gelu(gate_act, approximate=False) * up_act


def soft_router(logits):
    return jax.nn.softmax(logits, axis=-1)


def body(
    n_dp,
    n_t,
    tokens,
    cotangent,
    segment_ids,
    routes,
    buckets,
    gain_attn,
    w_query,
    w_key,
    w_value,
    w_out_t,
    gain_moe,
    w_router,
    w_gate,
    w_up,
    w_down_t,
    bias_table,
):
    seq, width = tokens.shape
    n_exp, d_rows, hidden = w_gate.shape
    n_heads, n_buckets = bias_table.shape
    cols = n_heads * DH
    cuts = n_dp // n_exp
    part = hidden // cuts
    sizes = {"dp": n_dp, "tensor": n_t}
    turn = lax.axis_index("tensor")
    SDS = jax.ShapeDtypeStruct

    packed = jnp.concatenate([w_query, w_key, w_value, w_out_t], axis=1)
    smalls = jnp.concatenate(
        [gain_attn[None], gain_moe[None], w_router.T, jnp.zeros((2, d_rows), BF)], axis=0
    )
    experts_out = [
        jnp.stack([w[:, :, c * part : (c + 1) * part] for c in range(cuts)], axis=1).reshape(
            n_dp, d_rows, part
        )
        for w in (w_gate, w_up, w_down_t)
    ]
    full, small_full = gather([packed, smalls], n_dp, 0)
    full = full.reshape(width, 4 * cols)
    w_qkv, w_out = full[:, : 3 * cols], full[:, 3 * cols :]
    small_full = small_full.transpose(1, 0, 2).reshape(8, width)
    attn_gain_f = small_full[0].astype(F32)
    moe_gain_f = small_full[1].astype(F32)
    router_t = small_full[2 : 2 + n_exp]

    token_f = tokens.astype(F32)
    normed = rms_scale(token_f, attn_gain_f).astype(BF)
    qkv = mm(normed, w_qkv).astype(BF)
    buckets_rev = jnp.roll(jnp.flip(buckets), 1)
    dist_hot = (buckets_rev[:, None] == jnp.arange(n_buckets, dtype=jnp.int32)[None, :]).astype(F32)
    dist_bias = jnp.dot(bias_table.astype(F32), dist_hot.T, precision=HIGHEST)
    mixed, prob = local_call(
        attn_fwd_kernel,
        [SDS((seq, cols), BF), SDS((n_heads, seq, seq), F32)],
        qkv,
        segment_ids,
        segment_ids.reshape(seq, 1),
        dist_bias,
    )
    attn_part = mm(mixed, w_out, 1, 1).astype(BF)
    attn_parts, *experts_in = exchange(
        sizes, [attn_part] + experts_out, (0, 1, 1, 1), ("tensor", "dp", "dp", "dp"), 1
    )
    e_gate, e_up, e_down = [w.reshape(width, part) for w in experts_in]
    residual = token_f + jnp.sum(attn_parts.astype(F32), axis=0)
    normed_moe = rms_scale(residual, moe_gain_f).astype(BF)
    logits = mm(normed_moe, router_t, 1, 1)
    router = soft_router(logits)

    expert_ids = jnp.arange(n_exp, dtype=jnp.int32)
    chosen = jnp.any(routes[:, :, None] == expert_ids[None, None, :], axis=1)
    chosen_b = chosen.astype(BF)
    position = jnp.arange(seq, dtype=jnp.int32)
    lower = (position[:, None] >= position[None, :]).astype(BF)
    place = mm(lower, chosen_b).astype(jnp.int32) - 1
    place = jnp.where(chosen, place, -1)
    slot_ids = jnp.arange(CAP, dtype=jnp.int32)
    pick = (place.T[:, None, :] == slot_ids[None, :, None]).astype(BF)
    gates = router * chosen.astype(F32)
    grad_final = cotangent.astype(F32)
    quarter = width // 2
    column = lax.rem(turn, 2) * quarter
    is_out = turn < 2
    grad_slice = lax.dynamic_slice_in_dim(grad_final, column, quarter, 1)
    moe_slice = lax.dynamic_slice_in_dim(normed_moe, column, quarter, 1)
    rows_all = jnp.where(is_out, moe_slice[None], (gates.T[:, :, None] * grad_slice[None]).astype(BF))
    sends = jnp.einsum("est,etd->esd", pick, rows_all, preferred_element_type=F32).astype(BF)
    arrived = dispatch(sends, n_dp, cuts, 2).reshape(4, n_dp * CAP, quarter)
    rows_x = jnp.concatenate([arrived[0], arrived[1]], axis=1)
    rows_d = jnp.concatenate([arrived[2], arrived[3]], axis=1)

    gate_act = mm(rows_x, e_gate)
    up_act = mm(rows_x, e_up)
    inner, unit_pull = jax.vjp(gated_unit, gate_act, up_act)
    inner = inner.astype(BF)
    d_inner = mm(rows_d, e_down)
    d_gate_act, d_up_act = unit_pull(d_inner)
    d_gate_act, d_up_act = d_gate_act.astype(BF), d_up_act.astype(BF)
    part_out = mm(inner, e_down, 1, 1).astype(BF)
    part_dx = (mm(d_gate_act, e_gate, 1, 1) + mm(d_up_act, e_up, 1, 1)).astype(BF)
    returns = jnp.stack(
        [p[:, c : c + quarter] for p in (part_out, part_dx) for c in (0, quarter)]
    ).reshape(4, n_dp, CAP, quarter)
    returned = send_home(returns, n_dp, 3)
    g_down = mm(rows_d, inner, 0, 0).astype(BF)
    g_gate = mm(rows_x, d_gate_act, 0, 0).astype(BF)
    g_up = mm(rows_x, d_up_act, 0, 0).astype(BF)

    returned = returned.reshape(n_exp, cuts * CAP, quarter)
    pick_back = jnp.tile(pick, (1, cuts, 1))
    home = jnp.einsum("est,esd->etd", pick_back, returned, preferred_element_type=F32)
    scaled = jnp.where(is_out, gates.T, 1.0)
    layer_part = jnp.sum(scaled[:, :, None] * home, axis=0).astype(BF)
    d_router_part = jnp.where(is_out, jnp.sum(home * grad_slice[None], axis=2), 0.0)
    g_exp = [g.reshape(n_dp, d_rows, part) for g in (g_gate, g_up, g_down)]
    layer_parts, d_router_parts, *r_exp = exchange(
        sizes,
        [layer_part, d_router_part] + g_exp,
        (0, 0, 1, 1, 1),
        ("tensor", "tensor", "dp", "dp", "dp"),
        4,
    )
    layer_parts = layer_parts.astype(F32)
    moe_out = jnp.concatenate([layer_parts[0], layer_parts[1]], axis=1)
    d_moe = jnp.concatenate([layer_parts[2], layer_parts[3]], axis=1)
    d_router = jnp.sum(d_router_parts, axis=0).T
    output = (residual + moe_out).astype(BF)

    unused, soft_pull = jax.vjp(soft_router, logits)
    d_logits = soft_pull(d_router)[0].astype(BF)
    g_router = mm(d_logits, normed_moe, 0, 0)
    d_normed_moe = d_moe + mm(d_logits, router_t)
    unused, moe_pull = jax.vjp(rms_scale, residual, moe_gain_f)
    d_resid_norm, g_moe_gain = moe_pull(d_normed_moe)
    d_residual = grad_final + d_resid_norm
    d_branch = d_residual.astype(BF)
    g_out = mm(d_branch, mixed, 0, 0)
    d_mixed = mm(d_branch, w_out).astype(BF)
    d_qkv, d_dist = local_call(
        attn_bwd_kernel,
        [SDS((seq, 3 * cols), BF), SDS((n_heads, seq), F32)],
        qkv,
        prob,
        d_mixed,
    )
    g_table = jnp.dot(d_dist, dist_hot, precision=HIGHEST)
    d_normed_part = mm(d_qkv, w_qkv, 1, 1).astype(BF)
    g_qkv = mm(normed, d_qkv, 0, 0)
    g_attn = jnp.concatenate([g_qkv, g_out], axis=1).astype(BF).reshape(n_dp, d_rows, 4 * cols)
    g_small = jnp.concatenate(
        [g_moe_gain[None], g_router, jnp.zeros((7 - n_exp, width), F32)], axis=0
    )
    g_small = g_small.reshape(8, n_dp, d_rows).transpose(1, 0, 2)
    d_normed_parts, r_small, r_table, r_attn = exchange(
        sizes,
        [d_normed_part, g_small, g_table],
        (0, 1, 0),
        ("tensor", "dp", "dp"),
        5,
        g_attn,
    )
    d_normed = jnp.sum(d_normed_parts.astype(F32), axis=0)
    unused, first_pull = jax.vjp(rms_scale, token_f, attn_gain_f)
    d_token_norm, g_attn_gain = first_pull(d_normed)
    grad_tokens = (d_residual + d_token_norm).astype(BF)
    (r_gain,) = exchange(sizes, [g_attn_gain.reshape(n_dp, 1, d_rows)], (1,), ("dp",), 6)
    attn_total = jnp.sum(r_attn.astype(F32), axis=0)
    small_total = jnp.sum(r_small, axis=0)
    exp_total = []
    for r in r_exp:
        r = r.reshape(n_exp, cuts, d_rows, part)
        exp_total.append(jnp.concatenate([r[:, c] for c in range(cuts)], axis=2).astype(F32))
    return (
        output,
        grad_tokens,
        jnp.sum(r_gain, axis=0)[0],
        attn_total[:, :cols],
        attn_total[:, cols : 2 * cols],
        attn_total[:, 2 * cols : 3 * cols],
        attn_total[:, 3 * cols :],
        small_total[0],
        small_total[1 : 1 + n_exp].T,
        exp_total[0],
        exp_total[1],
        exp_total[2],
        jnp.sum(r_table, axis=0),
    )


def solution(mesh):
    row, both, expert = P("dp", None), P("dp", "tensor"), P(None, "dp", "tensor")
    table = P("tensor", None)
    in_specs = (row, row, row, row, P(), P("dp"), both, both, both, both, P("dp"), row)
    in_specs = in_specs + (expert, expert, expert, table)
    out_specs = (row, row, P("dp"), both, both, both, both, P("dp"), row)
    out_specs = out_specs + (expert, expert, expert, table)
    return jax.shard_map(
        functools.partial(body, mesh.shape["dp"], mesh.shape["tensor"]),
        mesh=mesh,
        in_specs=in_specs,
        out_specs=out_specs,
        check_vma=False,
    )
```
